512 devices in a mesh: row: 8 (over x, y_lo), col: 16 (over z), dp: 4 (over y_hi, core).
Axes of the slice: x: 4, y: 4 (y_hi: 2, y_lo: 2; y = y_hi * 2 + y_lo), z: 16, core: 2. Of those that a mesh axis runs over, the one named last changes fastest.
Arguments:
- tokens: bfloat16 [512, 16384], P('dp', 'col'), may hold values from -6 to 6
- block_values: bfloat16 [8, 16, 32, 128, 128], P('row', 'col'), may hold values from -0.21875 to 0.21875
- block_index: int32 [8, 16, 2, 32], P('row', 'col'), may hold values from 0 to 31, as said below
- block_count: int32 [8, 16], P('row', 'col'), may hold values from 4 to 32, as said below
- grad_hidden: bfloat16 [512, 32768], P('dp', ('row', 'col')), may hold values from -3 to 3
Outputs:
- hidden: bfloat16 [512, 32768], P('dp', ('row', 'col'))
- grad_tokens: bfloat16 [512, 16384], P('dp', ('col', 'row'))
- grad_blocks: bfloat16 [8, 16, 32, 128, 128], P('row', 'col', 'dp')
The draws below stay inside these ranges and needn't reach their ends.
Inputs may be any that keep to these rules, and one draw needn't show every extreme that they name: block_index[r, c, 0, s] is a block row below 32 and block_index[r, c, 1, s] a block column below 8 inside cell (r, c); the live slots of a cell name distinct positions; slots at or past block_count[r, c] are unused. `block_count`: some cell holds exactly 32 live slots in every draw.
All inputs are finite; a program needn't handle non-finite values.
Results may differ from the reference program's by a relative error of at most 0.017.
Values may be sent and summed in bfloat16 or wider, within the bound.
No kernel may reach another device: no remote copies, remote signals or barrier semaphores. Data moves between devices by JAX's collectives and lax.ppermute only.
A program may use at most 64 MiB of HBM per device.

```python
import jax
import jax.numpy as jnp
from jax import lax

D = 16384
H = 32768
BLK = 128
CAP = 32
TOKENS = 512
HID_BLOCKS = 32
WID_BLOCKS = 8
N_ROW = 8
N_COL = 16


def cell_layout(key):
    cells = N_ROW * N_COL
    positions = HID_BLOCKS * WID_BLOCKS
    base_counts = jax.random.randint(jax.random.fold_in(key, 101), (cells,), CAP // 8, CAP // 2 + 1)
    ranking = jax.random.permutation(jax.random.fold_in(key, 102), cells)
    heavy_cells = max(1, cells // 16)
    counts = jnp.where(ranking < heavy_cells, CAP, base_counts)
    counts = jnp.where(ranking == heavy_cells, CAP // 8, counts)
    cell_keys = jax.random.split(jax.random.fold_in(key, 103), cells)

    def pick_cell(one_key):
        return jax.random.permutation(one_key, positions)[:CAP]
    chosen = jax.vmap(pick_cell)(cell_keys)
    block_rows = chosen // WID_BLOCKS
    block_cols = chosen % WID_BLOCKS
    layout = jnp.stack([block_rows, block_cols], axis=1).reshape(N_ROW, N_COL, 2, CAP)
    return (layout.astype(jnp.int32), counts.reshape(N_ROW, N_COL).astype(jnp.int32))


def draw_block_index(key, part):
    return cell_layout(key)[0]


def draw_block_count(key, part):
    return cell_layout(key)[1]


def block_levels(own_key, dims, shards, least, largest):
    level = 1.0
    for dim, blocks in shards:
        draws = jax.random.uniform(jax.random.fold_in(jax.random.fold_in(own_key, 6), dim), (blocks,), jnp.float32, least / len(shards), largest / len(shards))
        level = level * jnp.repeat(jnp.exp(draws), dims[dim] // blocks).reshape((-1,) + (1,) * (len(dims) - 1 - dim))
    return level


def gaussian(own_key, shape, deviation, reach, cuts=(), kind=jnp.bfloat16):
    gain = block_levels(own_key, shape, cuts, -0.22, 0.18) if cuts else 1.0
    result = jax.random.normal(own_key, shape, jnp.float32) * deviation * gain
    return jnp.minimum(jnp.maximum(result, -reach), reach).astype(kind)


def setup_inputs(seed: int = 0) -> dict:
    seeds = jax.random.split(jax.random.key(seed), 6)
    tokens = gaussian(seeds[0], (TOKENS, D), 1.0, 6.0, ((0, 4), (1, 16)))
    block_values = gaussian(seeds[1], (N_ROW, N_COL, CAP, BLK, BLK), (N_COL * CAP * BLK // (3 * HID_BLOCKS)) ** -0.5, 0.21875, ((0, 8), (1, 16)))
    block_index = draw_block_index(jax.random.fold_in(seeds[5], 71), 0)
    block_count = draw_block_count(jax.random.fold_in(seeds[5], 71), 0)
    grad_hidden = gaussian(seeds[4], (TOKENS, H), 0.5, 3.0, ((0, 4), (1, 128)))
    return dict(tokens=tokens, block_values=block_values, block_index=block_index, block_count=block_count, grad_hidden=grad_hidden)


grad_scale = 0.0625


def reference(tokens, block_values, block_index, block_count, grad_hidden):
    row_blocks = H // (BLK * N_ROW)
    col_blocks = D // (BLK * N_COL)
    token_cells = tokens.reshape(TOKENS, N_COL, col_blocks, BLK)
    grad_cells = grad_hidden.reshape(TOKENS, N_ROW, row_blocks, BLK)
    live_table = jnp.arange(CAP, dtype=jnp.int32)[None, None, :] < block_count[:, :, None]

    def cell_parts(row_id, col_id):
        weights = block_values[row_id, col_id].astype(jnp.float32)
        slot_rows = block_index[row_id, col_id, 0]
        slot_cols = block_index[row_id, col_id, 1]
        live_slots = live_table[row_id, col_id]
        token_pick = jnp.take(token_cells[:, col_id], slot_cols, axis=1).astype(jnp.float32)
        grad_pick = jnp.take(grad_cells[:, row_id], slot_rows, axis=1).astype(jnp.float32)
        return weights, slot_rows, slot_cols, live_slots, token_pick, grad_pick

    def hidden_row(row_id):
        def add_col(running, col_id):
            weights, slot_rows, slot_cols, live_slots, token_pick, grad_pick = cell_parts(row_id, col_id)
            slot_terms = jnp.einsum("tsm,snm->stn", token_pick, weights, precision=lax.Precision.HIGHEST)
            slot_terms = jnp.where(live_slots[:, None, None], slot_terms, 0.0)
            partial_sum = jax.ops.segment_sum(slot_terms, slot_rows, num_segments=row_blocks)
            rounded = lax.optimization_barrier(partial_sum.astype(jnp.bfloat16))
            return running + rounded.astype(jnp.float32), None

        initial = jnp.zeros((row_blocks, TOKENS, BLK), jnp.float32)
        totals = lax.scan(add_col, initial, jnp.arange(N_COL, dtype=jnp.int32))[0]
        return totals.astype(jnp.bfloat16)

    hidden_grid = lax.map(hidden_row, jnp.arange(N_ROW, dtype=jnp.int32))
    hidden = hidden_grid.transpose(2, 0, 1, 3).reshape(TOKENS, H)

    def grad_col(col_id):
        def add_row(running, row_id):
            weights, slot_rows, slot_cols, live_slots, token_pick, grad_pick = cell_parts(row_id, col_id)
            slot_terms = jnp.einsum("tsn,snm->stm", grad_pick, weights, precision=lax.Precision.HIGHEST)
            slot_terms = jnp.where(live_slots[:, None, None], slot_terms, 0.0)
            return running + jax.ops.segment_sum(slot_terms, slot_cols, num_segments=col_blocks), None

        initial = jnp.zeros((col_blocks, TOKENS, BLK), jnp.float32)
        totals = lax.scan(add_row, initial, jnp.arange(N_ROW, dtype=jnp.int32))[0]
        return totals.astype(jnp.bfloat16)

    grad_grid = lax.map(grad_col, jnp.arange(N_COL, dtype=jnp.int32))
    grad_tokens = grad_grid.transpose(2, 0, 1, 3).reshape(TOKENS, D)

    def weight_cell(cell_id):
        row_id = cell_id // N_COL
        col_id = cell_id % N_COL
        weights, slot_rows, slot_cols, live_slots, token_pick, grad_pick = cell_parts(row_id, col_id)
        sums = jnp.einsum("tsn,tsm->snm", grad_pick, token_pick, precision=lax.Precision.HIGHEST) * grad_scale
        return jnp.where(live_slots[:, None, None], sums, 0.0).astype(jnp.bfloat16)

    grad_blocks = lax.map(weight_cell, jnp.arange(N_ROW * N_COL, dtype=jnp.int32))
    grad_blocks = grad_blocks.reshape(N_ROW, N_COL, CAP, BLK, BLK)
    return hidden, grad_tokens, grad_blocks
```

```python
import jax
import jax.numpy as jnp
from jax import lax
from jax.experimental import pallas as pl
from jax.experimental.pallas import tpu as pltpu
from jax.sharding import PartitionSpec as P

grad_scale = 0.0625
block = 128
f32 = jnp.float32
bf16 = jnp.bfloat16


def hidden_kernel(
    index, live_count, plane, core_id, tokens, weights, own, up, down, far, token_blocks, total
):
    capacity = weights.shape[0]
    rows = total.shape[0] - 1
    for m in range(token_blocks.shape[0]):
        token_blocks[m] = tokens[:, m * block : (m + 1) * block]
    for b in range(rows):
        total[b] = jnp.zeros_like(total[b])
    count = live_count[0, 0]
    place = plane[0, 0]
    for s in range(capacity):
        live = s < count
        row = jnp.where(live, index[0, s], rows)
        col = jnp.where(live, index[1, s], 0)
        total[row] += lax.dot_general(
            token_blocks[col], weights[s], (((1,), (1,)), ((), ())), preferred_element_type=f32
        )
    for shift, out in ((1, up), (3, down), (2, far), (0, own)):
        near = lax.rem(place + shift, 4)
        for j in range(out.shape[0]):
            for half in range(2):
                out[j, :, half * block : (half + 1) * block] = total[
                    (j * 4 + near) * 2 + half
                ].astype(bf16)


def grads_kernel(
    index, live_count, plane, core_id, tokens, weights, own, above, below, far,
    features, keep, send, token_blocks, grads, total,
):
    capacity = weights.shape[0]
    cols = total.shape[0] - 1
    count = live_count[0, 0]
    place = plane[0, 0]
    core = core_id[0, 0]
    for m in range(cols):
        token_blocks[m] = tokens[:, m * block : (m + 1) * block]
        total[m] = jnp.zeros_like(total[m])
    for shift, part in ((0, own), (1, above), (3, below), (2, far)):
        near = lax.rem(place + shift, 4)
        for j in range(part.shape[0]):
            for half in range(2):
                grads[(j * 4 + near) * 2 + half] = part[j, :, half * block : (half + 1) * block]
    for n in range(capacity):
        group, other, spot = n % 16 // 8, n // 16, n % 8
        s = group * 16 + jnp.where(other == 0, 1 - core, core) * 8 + spot
        live = s < count
        row = jnp.where(live, index[0, s], 0)
        col = jnp.where(live, index[1, s], 0)
        picked = grads[row]
        product = lax.dot_general(
            picked, token_blocks[col], (((0,), (0,)), ((), ())), preferred_element_type=f32
        )
        out = send if other == 0 else keep
        out[group, spot] = jnp.where(live, product * grad_scale, 0.0).astype(bf16)
        total[jnp.where(live, col, cols)] += jnp.dot(
            picked, weights[s], preferred_element_type=f32
        )
    for m in range(cols):
        features[m] = total[m].astype(bf16)


def call(kernel, outs, scratch, flops, *operands):
    return pl.pallas_call(
        kernel,
        out_shape=[jax.ShapeDtypeStruct(s, bf16) for s in outs],
        in_specs=[pl.BlockSpec(memory_space=pltpu.SMEM)] * 4
        + [pl.BlockSpec(memory_space=pltpu.VMEM)] * (len(operands) - 4),
        out_specs=[pl.BlockSpec(memory_space=pltpu.VMEM)] * len(outs),
        scratch_shapes=[pltpu.VMEM(s, t) for s, t in scratch],
        compiler_params=pltpu.CompilerParams(vmem_limit_bytes=32 * 2**20),
        cost_estimate=pl.CostEstimate(flops=flops, bytes_accessed=2**22, transcendentals=0),
    )(*operands)


def shifted(x, axis, by):
    n = lax.axis_size(axis)
    return lax.ppermute(x, axis, [(i, (i + by) % n) for i in range(n)])


def both_ways(x, by):
    n, parts = lax.axis_size("col"), lax.axis_size("dp")
    pairs = []
    for i in range(n):
        for d in range(parts):
            to = (i + (by if d % 2 == 0 else -by)) % n
            pairs.append((i * parts + d, to * parts + d))
    return lax.ppermute(x, ("col", "dp"), pairs)


def swapped(x, axis, bit):
    return lax.ppermute(x, axis, [(i, i ^ bit) for i in range(lax.axis_size(axis))])


def summed(*parts):
    total = parts[0].astype(f32)
    for part in parts[1:]:
        total = total + part.astype(f32)
    return total.astype(bf16)


def local(tokens, block_values, block_index, block_count, grad_hidden):
    weights = block_values[0, 0]
    capacity = weights.shape[0]
    token_count = tokens.shape[0]
    col_blocks = tokens.shape[1] // block
    planes = lax.axis_size("col")
    rows = planes * (grad_hidden.shape[1] // block)
    place = lax.axis_index("col")
    dp = lax.axis_index("dp")
    core, side = lax.rem(dp, 2), lax.div(dp, 2)
    strided = [[i + 4 * j for j in range(planes // 4)] for i in range(4)]
    quarter = (planes // 4, token_count, grad_hidden.shape[1])
    info = (block_index[0, 0], block_count, place.reshape(1, 1), core.reshape(1, 1))
    blocks = (token_count, block)

    grads_own = lax.all_to_all(
        jnp.broadcast_to(grad_hidden[None], quarter), "col", 0, 0, tiled=True,
        axis_index_groups=strided,
    )
    own, up, down, far = call(
        hidden_kernel,
        [quarter] * 4,
        [((col_blocks, *blocks), bf16), ((rows + 1, *blocks), f32)],
        2 * capacity * token_count * block * block,
        *info, tokens, weights,
    )
    from_below = shifted(up, "col", 1)
    from_above = shifted(down, "col", -1)
    from_far = both_ways(far, 2)
    hidden_near = summed(own, from_below, from_above, from_far)
    grads_own, hidden_near = lax.optimization_barrier((grads_own, hidden_near))
    hidden_parts = lax.all_to_all(hidden_near, "col", 0, 0, tiled=True, axis_index_groups=strided)
    above = shifted(grads_own, "col", -1)
    below = shifted(grads_own, "col", 1)
    across = both_ways(grads_own, 2)

    features, keep, send = call(
        grads_kernel,
        [(col_blocks, *blocks), (2, 8, block, block), (2, 8, block, block)],
        [((col_blocks, *blocks), bf16), ((rows, *blocks), bf16), ((col_blocks + 1, *blocks), f32)],
        4 * capacity * token_count * block * block,
        *info, tokens, weights, grads_own, above, below, across,
    )
    features, send, hidden_parts = lax.optimization_barrier((features, send, hidden_parts))
    chip = summed(keep, swapped(send, "dp", 1))
    feature_parts = lax.all_to_all(features, "row", 0, 0, tiled=True)
    mine = lax.dynamic_index_in_dim(chip, side, 0, keepdims=False)
    theirs = lax.dynamic_index_in_dim(chip, 1 - side, 0, keepdims=False)
    grad_blocks = summed(mine, swapped(theirs, "dp", 2))
    grad_tokens = summed(*[feature_parts[i] for i in range(feature_parts.shape[0])])
    hidden = summed(*[hidden_parts[i] for i in range(planes // 4)])
    return hidden, grad_tokens, grad_blocks[None, None]


def solution(mesh):
    in_specs = (
        P("dp", "col"),
        P("row", "col", None, None, None),
        P("row", "col", None, None),
        P("row", "col"),
        P("dp", ("row", "col")),
    )
    out_specs = (
        P("dp", ("row", "col")),
        P("dp", ("col", "row")),
        P("row", "col", "dp", None, None),
    )
    return jax.shard_map(local, mesh=mesh, in_specs=in_specs, out_specs=out_specs, check_vma=False)
```

```python
import jax
import jax.numpy as jnp
from jax import lax
from jax.experimental import pallas as pl
from jax.experimental.pallas import tpu as pltpu
from jax.sharding import PartitionSpec as P

grad_scale = 0.0625
low_cost = 1000
high_cost = 8 * 10**9
block = 128
f32 = jnp.float32
bf16 = jnp.bfloat16


def hidden_kernel(
    index, live_count, plane, dp_place, tokens, weights, own, up, down, far, token_blocks, total
):
    capacity = weights.shape[0]
    rows = total.shape[0] - 1
    for m in range(token_blocks.shape[0]):
        token_blocks[m] = tokens[:, m * block : (m + 1) * block]
    for b in range(rows):
        total[b] = jnp.zeros_like(total[b])
    count = live_count[0, 0]
    place = plane[0, 0]
    for s in range(capacity):
        live = s < count
        row = jnp.where(live, index[0, s], rows)
        col = jnp.where(live, index[1, s], 0)
        total[row] += lax.dot_general(
            token_blocks[col], weights[s], (((1,), (1,)), ((), ())), preferred_element_type=f32
        )
    far_shift = 2 - 4 * lax.rem(dp_place[0, 0], 2)
    for shift, out in ((1, up), (-1, down), (far_shift, far), (0, own)):
        near = lax.rem(place + shift + 4, 4)
        for a in range(out.shape[0]):
            to = 4 * a + near
            for half in range(2):
                out[a, :, half * block : (half + 1) * block] = total[to * 2 + half].astype(bf16)


def gather_blocks(plane, dp_place, tokens, parts, token_blocks, grads):
    rows = grads.shape[0]
    for m in range(token_blocks.shape[0]):
        token_blocks[m] = tokens[:, m * block : (m + 1) * block]
    far_shift = 4 * lax.rem(dp_place[0, 0], 2) - 2
    for shift, part in zip((0, 1, -1, far_shift), parts):
        near = lax.rem(plane[0, 0] + shift + 4, 4)
        for a in range(part.shape[0]):
            at = 4 * a + near
            for half in range(2):
                grads[at * 2 + half] = part[a, :, half * block : (half + 1) * block]


def blocks_kernel(
    index, live_count, plane, dp_place, tokens, own, above, below, far,
    keep, keep_far, send, token_blocks, grads,
):
    gather_blocks(plane, dp_place, tokens, (own, above, below, far), token_blocks, grads)
    count = live_count[0, 0]
    core = lax.rem(dp_place[0, 0], 2)
    side = lax.div(dp_place[0, 0], 2)
    for n in range(index.shape[1]):
        from_core, from_side, spot = n // 16, n % 16 // 8, n % 8
        owner_core = core if from_core else 1 - core
        owner_side = side if from_side else 1 - side
        s = (owner_side * 2 + owner_core) * 8 + spot
        live = s < count
        product = lax.dot_general(
            grads[jnp.where(live, index[0, s], 0)],
            token_blocks[jnp.where(live, index[1, s], 0)],
            (((0,), (0,)), ((), ())),
            preferred_element_type=f32,
        )
        out = (keep if from_side else keep_far) if from_core else send.at[from_side]
        out[spot] = jnp.where(live, product * grad_scale, 0.0).astype(bf16)


def features_kernel(
    index, live_count, plane, dp_place, tokens, weights, own, above, below, far,
    features, token_blocks, grads, total,
):
    gather_blocks(plane, dp_place, tokens, (own, above, below, far), token_blocks, grads)
    cols = total.shape[0] - 1
    for m in range(cols):
        total[m] = jnp.zeros_like(total[m])
    for s in range(index.shape[1]):
        live = s < live_count[0, 0]
        total[jnp.where(live, index[1, s], cols)] += jnp.dot(
            grads[jnp.where(live, index[0, s], 0)], weights[s], preferred_element_type=f32
        )
    for m in range(cols):
        features[m] = total[m].astype(bf16)


def call(kernel, outs, scratch, flops, *operands):
    return pl.pallas_call(
        kernel,
        out_shape=[jax.ShapeDtypeStruct(s, bf16) for s in outs],
        in_specs=[pl.BlockSpec(memory_space=pltpu.SMEM)] * 4
        + [pl.BlockSpec(memory_space=pltpu.VMEM)] * (len(operands) - 4),
        out_specs=[pl.BlockSpec(memory_space=pltpu.VMEM)] * len(outs),
        scratch_shapes=[pltpu.VMEM(s, t) for s, t in scratch],
        compiler_params=pltpu.CompilerParams(vmem_limit_bytes=32 * 2**20),
        cost_estimate=pl.CostEstimate(flops=flops, bytes_accessed=flops // 256, transcendentals=0),
    )(*operands)


def sum_kernel(parts, out):
    total = parts[0].astype(f32)
    for n in range(1, parts.shape[0]):
        total += parts[n].astype(f32)
    out[...] = total.astype(bf16)


def call_sum(parts, flops):
    return pl.pallas_call(
        sum_kernel,
        out_shape=jax.ShapeDtypeStruct(parts.shape[1:], bf16),
        in_specs=[pl.BlockSpec(memory_space=pltpu.VMEM)],
        out_specs=pl.BlockSpec(memory_space=pltpu.VMEM),
        compiler_params=pltpu.CompilerParams(vmem_limit_bytes=8 * 2**20),
        cost_estimate=pl.CostEstimate(flops=flops, bytes_accessed=flops // 256, transcendentals=0),
    )(parts)


def shifted(x, axis, by):
    n = lax.axis_size(axis)
    return lax.ppermute(x, axis, [(i, (i + by) % n) for i in range(n)])


def both_ways(x, by):
    n, parts = lax.axis_size("col"), lax.axis_size("dp")
    pairs = []
    for i in range(n):
        for d in range(parts):
            to = (i + (by if d % 2 == 0 else -by)) % n
            pairs.append((i * parts + d, to * parts + d))
    return lax.ppermute(x, ("col", "dp"), pairs)


def swapped(x, axis, bit):
    return lax.ppermute(x, axis, [(i, i ^ bit) for i in range(lax.axis_size(axis))])


def summed(*parts):
    total = parts[0].astype(f32)
    for part in parts[1:]:
        total = total + part.astype(f32)
    return total.astype(bf16)


def local(tokens, block_values, block_index, block_count, grad_hidden):
    weights = block_values[0, 0]
    capacity = weights.shape[0]
    token_count = tokens.shape[0]
    col_blocks = tokens.shape[1] // block
    planes = lax.axis_size("col")
    rows = planes * (grad_hidden.shape[1] // block)
    place = lax.axis_index("col")
    dp = lax.axis_index("dp")
    quarter = (planes // 4, token_count, grad_hidden.shape[1])
    info = (block_index[0, 0], block_count, place.reshape(1, 1), dp.reshape(1, 1))
    blocks = (token_count, block)
    owned = (capacity // lax.axis_size("dp"), block, block)

    strided = [[i + 4 * j for j in range(planes // 4)] for i in range(4)]
    copies = jnp.broadcast_to(grad_hidden[None], quarter)
    grads_own = lax.all_to_all(copies, "col", 0, 0, tiled=True, axis_index_groups=strided)
    own, up, down, far = call(
        hidden_kernel,
        [quarter] * 4,
        [((col_blocks, *blocks), bf16), ((rows + 1, *blocks), f32)],
        2 * capacity * token_count * block * block,
        *info, tokens, weights,
    )
    from_below = shifted(up, "col", 1)
    from_above = shifted(down, "col", -1)
    from_far = both_ways(far, 2)
    hidden_near = summed(own, from_below, from_above, from_far)
    grads_own, hidden_near = lax.optimization_barrier((grads_own, hidden_near))
    hidden_parts = lax.all_to_all(hidden_near, "col", 0, 0, tiled=True, axis_index_groups=strided)
    above = shifted(grads_own, "col", -1)
    below = shifted(grads_own, "col", 1)
    across = both_ways(grads_own, 2)
    token_scratch = ((col_blocks, *blocks), bf16)
    grads_scratch = ((rows, *blocks), bf16)
    keep, keep_far, send = call(
        blocks_kernel,
        [owned, owned, (2, *owned)],
        [token_scratch, grads_scratch],
        low_cost,
        *info, tokens, grads_own, above, below, across,
    )
    received = swapped(send, "dp", 1)
    theirs = summed(keep_far, received[0])
    from_side = swapped(theirs, "dp", 2)
    [features] = call(
        features_kernel,
        [(col_blocks, *blocks)],
        [token_scratch, grads_scratch, ((col_blocks + 1, *blocks), f32)],
        low_cost,
        *info, tokens, weights, grads_own, above, below, across,
    )
    hidden = call_sum(hidden_parts, high_cost)
    features, from_side, hidden = lax.optimization_barrier((features, from_side, hidden))
    feature_parts = lax.all_to_all(features, "row", 0, 0, tiled=True)
    grad_blocks = summed(keep, received[1], from_side)
    grad_tokens = summed(*[feature_parts[i] for i in range(feature_parts.shape[0])])
    return hidden, grad_tokens, grad_blocks[None, None]


def solution(mesh):
    in_specs = (
        P("dp", "col"),
        P("row", "col", None, None, None),
        P("row", "col", None, None),
        P("row", "col"),
        P("dp", ("row", "col")),
    )
    out_specs = (
        P("dp", ("row", "col")),
        P("dp", ("col", "row")),
        P("row", "col", "dp", None, None),
    )
    return jax.shard_map(local, mesh=mesh, in_specs=in_specs, out_specs=out_specs, check_vma=False)
```

```python
import jax
import jax.numpy as jnp
from jax import lax
from jax.experimental import pallas as pl
from jax.experimental.pallas import tpu as pltpu
from jax.sharding import PartitionSpec as P

grad_scale = 0.0625
low_cost = 1000
high_cost = 8 * 10**9
block = 128
f32 = jnp.float32
bf16 = jnp.bfloat16


def hidden_kernel(
    index, live_count, plane, dp_place, tokens, weights, own, up, down, far, token_blocks, total
):
    capacity = weights.shape[0]
    rows = total.shape[0] - 1
    for m in range(token_blocks.shape[0]):
        token_blocks[m] = tokens[:, m * block : (m + 1) * block]
    for b in range(rows):
        total[b] = jnp.zeros_like(total[b])
    count = live_count[0, 0]
    place = plane[0, 0]
    for s in range(capacity):
        live = s < count
        row = jnp.where(live, index[0, s], rows)
        col = jnp.where(live, index[1, s], 0)
        total[row] += lax.dot_general(
            token_blocks[col], weights[s], (((1,), (1,)), ((), ())), preferred_element_type=f32
        )
    far_shift = 2 - 4 * lax.rem(dp_place[0, 0], 2)
    for shift, out in ((1, up), (-1, down), (far_shift, far), (0, own)):
        near = lax.rem(place + shift + 4, 4)
        for a in range(out.shape[0]):
            to = 4 * a + near
            for half in range(2):
                out[a, :, half * block : (half + 1) * block] = total[to * 2 + half].astype(bf16)


def gather_blocks(plane, dp_place, tokens, parts, token_blocks, grads):
    rows = grads.shape[0]
    for m in range(token_blocks.shape[0]):
        token_blocks[m] = tokens[:, m * block : (m + 1) * block]
    far_shift = 4 * lax.rem(dp_place[0, 0], 2) - 2
    for shift, part in zip((0, 1, -1, far_shift), parts):
        near = lax.rem(plane[0, 0] + shift + 4, 4)
        for a in range(part.shape[0]):
            at = 4 * a + near
            for half in range(2):
                grads[at * 2 + half] = part[a, :, half * block : (half + 1) * block]


def blocks_kernel(
    index, live_count, plane, dp_place, tokens, own, above, below, far,
    keep, keep_far, send, token_blocks, grads,
):
    gather_blocks(plane, dp_place, tokens, (own, above, below, far), token_blocks, grads)
    count = live_count[0, 0]
    core = lax.rem(dp_place[0, 0], 2)
    side = lax.div(dp_place[0, 0], 2)
    for n in range(index.shape[1]):
        from_core, from_side, spot = n // 16, n % 16 // 8, n % 8
        owner_core = core if from_core else 1 - core
        owner_side = side if from_side else 1 - side
        s = (owner_side * 2 + owner_core) * 8 + spot
        live = s < count
        product = lax.dot_general(
            grads[jnp.where(live, index[0, s], 0)],
            token_blocks[jnp.where(live, index[1, s], 0)],
            (((0,), (0,)), ((), ())),
            preferred_element_type=f32,
        )
        out = (keep if from_side else keep_far) if from_core else send.at[from_side]
        out[spot] = jnp.where(live, product * grad_scale, 0.0).astype(bf16)


def features_kernel(
    index, live_count, plane, dp_place, tokens, weights, own, above, below, far,
    features, token_blocks, grads, total,
):
    gather_blocks(plane, dp_place, tokens, (own, above, below, far), token_blocks, grads)
    cols = total.shape[0] - 1
    for m in range(cols):
        total[m] = jnp.zeros_like(total[m])
    for s in range(index.shape[1]):
        live = s < live_count[0, 0]
        total[jnp.where(live, index[1, s], cols)] += jnp.dot(
            grads[jnp.where(live, index[0, s], 0)], weights[s], preferred_element_type=f32
        )
    for m in range(cols):
        features[m] = total[m].astype(bf16)


def call(kernel, outs, scratch, flops, *operands):
    return pl.pallas_call(
        kernel,
        out_shape=[jax.ShapeDtypeStruct(s, bf16) for s in outs],
        in_specs=[pl.BlockSpec(memory_space=pltpu.SMEM)] * 4
        + [pl.BlockSpec(memory_space=pltpu.VMEM)] * (len(operands) - 4),
        out_specs=[pl.BlockSpec(memory_space=pltpu.VMEM)] * len(outs),
        scratch_shapes=[pltpu.VMEM(s, t) for s, t in scratch],
        compiler_params=pltpu.CompilerParams(vmem_limit_bytes=32 * 2**20),
        cost_estimate=pl.CostEstimate(flops=flops, bytes_accessed=flops // 256, transcendentals=0),
    )(*operands)


def sum_kernel(parts, out):
    total = parts[0].astype(f32)
    for n in range(1, parts.shape[0]):
        total += parts[n].astype(f32)
    out[...] = total.astype(bf16)


def call_sum(parts, flops):
    return pl.pallas_call(
        sum_kernel,
        out_shape=jax.ShapeDtypeStruct(parts.shape[1:], bf16),
        in_specs=[pl.BlockSpec(memory_space=pltpu.VMEM)],
        out_specs=pl.BlockSpec(memory_space=pltpu.VMEM),
        compiler_params=pltpu.CompilerParams(vmem_limit_bytes=8 * 2**20),
        cost_estimate=pl.CostEstimate(flops=flops, bytes_accessed=flops // 256, transcendentals=0),
    )(parts)


def shifted(x, axis, by):
    n = lax.axis_size(axis)
    return lax.ppermute(x, axis, [(i, (i + by) % n) for i in range(n)])


def both_ways(x, by):
    n, parts = lax.axis_size("col"), lax.axis_size("dp")
    pairs = []
    for i in range(n):
        for d in range(parts):
            to = (i + (by if d % 2 == 0 else -by)) % n
            pairs.append((i * parts + d, to * parts + d))
    return lax.ppermute(x, ("col", "dp"), pairs)


def swapped(x, axis, bit):
    return lax.ppermute(x, axis, [(i, i ^ bit) for i in range(lax.axis_size(axis))])


def summed(*parts):
    total = parts[0].astype(f32)
    for part in parts[1:]:
        total = total + part.astype(f32)
    return total.astype(bf16)


def local(tokens, block_values, block_index, block_count, grad_hidden):
    weights = block_values[0, 0]
    capacity = weights.shape[0]
    token_count = tokens.shape[0]
    col_blocks = tokens.shape[1] // block
    planes = lax.axis_size("col")
    rows = planes * (grad_hidden.shape[1] // block)
    place = lax.axis_index("col")
    dp = lax.axis_index("dp")
    quarter = (planes // 4, token_count, grad_hidden.shape[1])
    info = (block_index[0, 0], block_count, place.reshape(1, 1), dp.reshape(1, 1))
    blocks = (token_count, block)
    owned = (capacity // lax.axis_size("dp"), block, block)

    strided = [[i + 4 * j for j in range(planes // 4)] for i in range(4)]
    copies = jnp.broadcast_to(grad_hidden[None], quarter)
    grads_own = lax.all_to_all(copies, "col", 0, 0, tiled=True, axis_index_groups=strided)
    own, up, down, far = call(
        hidden_kernel,
        [quarter] * 4,
        [((col_blocks, *blocks), bf16), ((rows + 1, *blocks), f32)],
        2 * capacity * token_count * block * block,
        *info, tokens, weights,
    )
    from_below = shifted(up, "col", 1)
    from_above = shifted(down, "col", -1)
    from_far = both_ways(far, 2)
    grads_own, from_below, from_above, from_far = lax.optimization_barrier(
        (grads_own, from_below, from_above, from_far)
    )
    hidden_near = summed(own, from_below, from_above, from_far)
    hidden_parts = lax.all_to_all(hidden_near, "col", 0, 0, tiled=True, axis_index_groups=strided)
    above = shifted(grads_own, "col", -1)
    below = shifted(grads_own, "col", 1)
    across = both_ways(grads_own, 2)
    token_scratch = ((col_blocks, *blocks), bf16)
    grads_scratch = ((rows, *blocks), bf16)
    keep, keep_far, send = call(
        blocks_kernel,
        [owned, owned, (2, *owned)],
        [token_scratch, grads_scratch],
        low_cost,
        *info, tokens, grads_own, above, below, across,
    )
    received = swapped(send, "dp", 1)
    theirs = summed(keep_far, received[0])
    from_side = swapped(theirs, "dp", 2)
    [features] = call(
        features_kernel,
        [(col_blocks, *blocks)],
        [token_scratch, grads_scratch, ((col_blocks + 1, *blocks), f32)],
        low_cost,
        *info, tokens, weights, grads_own, above, below, across,
    )
    hidden = call_sum(hidden_parts, high_cost)
    features, from_side, hidden = lax.optimization_barrier((features, from_side, hidden))
    feature_parts = lax.all_to_all(features, "row", 0, 0, tiled=True)
    grad_blocks = summed(keep, received[1], from_side)
    grad_tokens = summed(*[feature_parts[i] for i in range(feature_parts.shape[0])])
    return hidden, grad_tokens, grad_blocks[None, None]


def solution(mesh):
    in_specs = (
        P("dp", "col"),
        P("row", "col", None, None, None),
        P("row", "col", None, None),
        P("row", "col"),
        P("dp", ("row", "col")),
    )
    out_specs = (
        P("dp", ("row", "col")),
        P("dp", ("col", "row")),
        P("row", "col", "dp", None, None),
    )
    return jax.shard_map(local, mesh=mesh, in_specs=in_specs, out_specs=out_specs, check_vma=False)
```

```python
import jax
import jax.numpy as jnp
from jax import lax
from jax.experimental import pallas as pl
from jax.experimental.pallas import tpu as pltpu
from jax.sharding import PartitionSpec as P

grad_scale = 0.0625
low_cost = 1000
high_cost = 8 * 10**9
block = 128
f32 = jnp.float32
bf16 = jnp.bfloat16


def hidden_kernel(
    index, live_count, plane, dp_place, tokens, weights, own, up, down, far, token_blocks, total
):
    capacity = weights.shape[0]
    rows = total.shape[0] - 1
    for m in range(token_blocks.shape[0]):
        token_blocks[m] = tokens[:, m * block : (m + 1) * block]
    for b in range(rows):
        total[b] = jnp.zeros_like(total[b])
    count = live_count[0, 0]
    place = plane[0, 0]
    for s in range(capacity):
        live = s < count
        row = jnp.where(live, index[0, s], rows)
        col = jnp.where(live, index[1, s], 0)
        total[row] += lax.dot_general(
            token_blocks[col], weights[s], (((1,), (1,)), ((), ())), preferred_element_type=f32
        )
    far_shift = 2 - 4 * lax.rem(dp_place[0, 0], 2)
    for shift, out in ((1, up), (-1, down), (far_shift, far), (0, own)):
        near = lax.rem(place + shift + 4, 4)
        for a in range(out.shape[0]):
            to = 4 * a + near
            for half in range(2):
                out[a, :, half * block : (half + 1) * block] = total[to * 2 + half].astype(bf16)


def gather_blocks(plane, dp_place, tokens, parts, token_blocks, grads):
    rows = grads.shape[0]
    for m in range(token_blocks.shape[0]):
        token_blocks[m] = tokens[:, m * block : (m + 1) * block]
    far_shift = 4 * lax.rem(dp_place[0, 0], 2) - 2
    for shift, part in zip((0, 1, -1, far_shift), parts):
        near = lax.rem(plane[0, 0] + shift + 4, 4)
        for a in range(part.shape[0]):
            at = 4 * a + near
            for half in range(2):
                grads[at * 2 + half] = part[a, :, half * block : (half + 1) * block]


def blocks_kernel(
    index, live_count, plane, dp_place, tokens, own, above, below, far,
    keep, keep_far, send, token_blocks, grads,
):
    gather_blocks(plane, dp_place, tokens, (own, above, below, far), token_blocks, grads)
    count = live_count[0, 0]
    core = lax.rem(dp_place[0, 0], 2)
    side = lax.div(dp_place[0, 0], 2)
    for n in range(index.shape[1]):
        from_core, from_side, spot = n // 16, n % 16 // 8, n % 8
        owner_core = core if from_core else 1 - core
        owner_side = side if from_side else 1 - side
        s = (owner_side * 2 + owner_core) * 8 + spot
        live = s < count
        product = lax.dot_general(
            grads[jnp.where(live, index[0, s], 0)],
            token_blocks[jnp.where(live, index[1, s], 0)],
            (((0,), (0,)), ((), ())),
            preferred_element_type=f32,
        )
        out = (keep if from_side else keep_far) if from_core else send.at[from_side]
        out[spot] = jnp.where(live, product * grad_scale, 0.0).astype(bf16)


def features_kernel(
    index, live_count, plane, dp_place, tokens, weights, own, above, below, far,
    kept, sent, token_blocks, grads, total,
):
    gather_blocks(plane, dp_place, tokens, (own, above, below, far), token_blocks, grads)
    cols = total.shape[0] - 1
    for m in range(cols):
        total[m] = jnp.zeros_like(total[m])
    for s in range(index.shape[1]):
        live = s < live_count[0, 0]
        total[jnp.where(live, index[1, s], cols)] += jnp.dot(
            grads[jnp.where(live, index[0, s], 0)], weights[s], preferred_element_type=f32
        )
    here = lax.rem(dp_place[0, 1], 2)
    for k in range(cols // 2):
        kept[k] = total[2 * k + here].astype(bf16)
        sent[k] = total[2 * k + 1 - here].astype(bf16)


def call(kernel, outs, scratch, flops, *operands):
    return pl.pallas_call(
        kernel,
        out_shape=[jax.ShapeDtypeStruct(s, bf16) for s in outs],
        in_specs=[pl.BlockSpec(memory_space=pltpu.SMEM)] * 4
        + [pl.BlockSpec(memory_space=pltpu.VMEM)] * (len(operands) - 4),
        out_specs=[pl.BlockSpec(memory_space=pltpu.VMEM)] * len(outs),
        scratch_shapes=[pltpu.VMEM(s, t) for s, t in scratch],
        compiler_params=pltpu.CompilerParams(vmem_limit_bytes=32 * 2**20),
        cost_estimate=pl.CostEstimate(flops=flops, bytes_accessed=flops // 256, transcendentals=0),
    )(*operands)


def sum_kernel(parts, out):
    total = parts[0].astype(f32)
    for n in range(1, parts.shape[0]):
        total += parts[n].astype(f32)
    out[...] = total.astype(bf16)


def call_sum(parts, flops):
    return pl.pallas_call(
        sum_kernel,
        out_shape=jax.ShapeDtypeStruct(parts.shape[1:], bf16),
        in_specs=[pl.BlockSpec(memory_space=pltpu.VMEM)],
        out_specs=pl.BlockSpec(memory_space=pltpu.VMEM),
        compiler_params=pltpu.CompilerParams(vmem_limit_bytes=8 * 2**20),
        cost_estimate=pl.CostEstimate(flops=flops, bytes_accessed=flops // 256, transcendentals=0),
    )(parts)


def shifted(x, axis, by):
    n = lax.axis_size(axis)
    return lax.ppermute(x, axis, [(i, (i + by) % n) for i in range(n)])


def both_ways(x, by):
    n, parts = lax.axis_size("col"), lax.axis_size("dp")
    pairs = []
    for i in range(n):
        for d in range(parts):
            to = (i + (by if d % 2 == 0 else -by)) % n
            pairs.append((i * parts + d, to * parts + d))
    return lax.ppermute(x, ("col", "dp"), pairs)


def swapped(x, axis, bit):
    return lax.ppermute(x, axis, [(i, i ^ bit) for i in range(lax.axis_size(axis))])


def summed(*parts):
    total = parts[0].astype(f32)
    for part in parts[1:]:
        total = total + part.astype(f32)
    return total.astype(bf16)


def local(tokens, block_values, block_index, block_count, grad_hidden):
    weights = block_values[0, 0]
    capacity = weights.shape[0]
    token_count = tokens.shape[0]
    col_blocks = tokens.shape[1] // block
    planes = lax.axis_size("col")
    rows = planes * (grad_hidden.shape[1] // block)
    place = lax.axis_index("col")
    dp = lax.axis_index("dp")
    quarter = (planes // 4, token_count, grad_hidden.shape[1])
    info = (block_index[0, 0], block_count, place.reshape(1, 1), jnp.stack([dp, lax.axis_index("row")])[None])
    blocks = (token_count, block)
    owned = (capacity // lax.axis_size("dp"), block, block)

    strided = [[i + 4 * j for j in range(planes // 4)] for i in range(4)]
    copies = jnp.broadcast_to(grad_hidden[None], quarter)
    grads_own = lax.all_to_all(copies, "col", 0, 0, tiled=True, axis_index_groups=strided)
    own, up, down, far = call(
        hidden_kernel,
        [quarter] * 4,
        [((col_blocks, *blocks), bf16), ((rows + 1, *blocks), f32)],
        2 * capacity * token_count * block * block,
        *info, tokens, weights,
    )
    from_below = shifted(up, "col", 1)
    from_above = shifted(down, "col", -1)
    from_far = both_ways(far, 2)
    grads_own, from_below, from_above, from_far = lax.optimization_barrier(
        (grads_own, from_below, from_above, from_far)
    )
    hidden_near = summed(own, from_below, from_above, from_far)
    hidden_parts = lax.all_to_all(hidden_near, "col", 0, 0, tiled=True, axis_index_groups=strided)
    above = shifted(grads_own, "col", -1)
    below = shifted(grads_own, "col", 1)
    across = both_ways(grads_own, 2)
    token_scratch = ((col_blocks, *blocks), bf16)
    grads_scratch = ((rows, *blocks), bf16)
    keep, keep_far, send = call(
        blocks_kernel,
        [owned, owned, (2, *owned)],
        [token_scratch, grads_scratch],
        low_cost,
        *info, tokens, grads_own, above, below, across,
    )
    received = swapped(send, "dp", 1)
    theirs = summed(keep_far, received[0])
    from_side = swapped(theirs, "dp", 2)
    kept, sent = call(
        features_kernel,
        [(col_blocks // 2, *blocks)] * 2,
        [token_scratch, grads_scratch, ((col_blocks + 1, *blocks), f32)],
        low_cost,
        *info, tokens, weights, grads_own, above, below, across,
    )
    features = summed(kept, swapped(sent, "row", 1))
    hidden = call_sum(hidden_parts, high_cost)
    features, hidden = lax.optimization_barrier((features, hidden))
    along_x = [list(range(i, col_blocks, 2)) for i in range(2)]
    feature_parts = lax.all_to_all(
        features, "row", 0, 0, tiled=True, axis_index_groups=along_x
    )
    grad_blocks = summed(keep, received[1], from_side)
    feature_parts, grad_blocks = lax.optimization_barrier((feature_parts, grad_blocks))
    grad_tokens = summed(*[feature_parts[i] for i in range(feature_parts.shape[0])])
    return hidden, grad_tokens, grad_blocks[None, None]


def solution(mesh):
    in_specs = (
        P("dp", "col"),
        P("row", "col", None, None, None),
        P("row", "col", None, None),
        P("row", "col"),
        P("dp", ("row", "col")),
    )
    out_specs = (
        P("dp", ("row", "col")),
        P("dp", ("col", "row")),
        P("row", "col", "dp", None, None),
    )
    return jax.shard_map(local, mesh=mesh, in_specs=in_specs, out_specs=out_specs, check_vma=False)
```

```python
import jax
import jax.numpy as jnp
from jax import lax
from jax.experimental import pallas as pl
from jax.experimental.pallas import tpu as pltpu
from jax.sharding import PartitionSpec as P

grad_scale = 0.0625
low_cost = 1000
high_cost = 8 * 10**9
block = 128
f32 = jnp.float32
bf16 = jnp.bfloat16


def hidden_kernel(
    index, live_count, plane, dp_place, tokens, weights, own, up, down, far, token_blocks, total
):
    capacity = weights.shape[0]
    rows = total.shape[0] - 1
    for m in range(token_blocks.shape[0]):
        token_blocks[m] = tokens[:, m * block : (m + 1) * block]
    for b in range(rows):
        total[b] = jnp.zeros_like(total[b])
    count = live_count[0, 0]
    place = plane[0, 0]
    for s in range(capacity):
        live = s < count
        row = jnp.where(live, index[0, s], rows)
        col = jnp.where(live, index[1, s], 0)
        total[row] += lax.dot_general(
            token_blocks[col], weights[s], (((1,), (1,)), ((), ())), preferred_element_type=f32
        )
    far_shift = 2 - 4 * lax.rem(dp_place[0, 0], 2)
    for shift, out in ((1, up), (-1, down), (far_shift, far), (0, own)):
        near = lax.rem(place + shift + 4, 4)
        for a in range(out.shape[0]):
            to = 4 * a + near
            for half in range(2):
                out[a, :, half * block : (half + 1) * block] = total[to * 2 + half].astype(bf16)


def gather_blocks(plane, dp_place, tokens, parts, token_blocks, grads):
    rows = grads.shape[0]
    for m in range(token_blocks.shape[0]):
        token_blocks[m] = tokens[:, m * block : (m + 1) * block]
    far_shift = 4 * lax.rem(dp_place[0, 0], 2) - 2
    for shift, part in zip((0, 1, -1, far_shift), parts):
        near = lax.rem(plane[0, 0] + shift + 4, 4)
        for a in range(part.shape[0]):
            at = 4 * a + near
            for half in range(2):
                grads[at * 2 + half] = part[a, :, half * block : (half + 1) * block]


def blocks_kernel(
    index, live_count, plane, dp_place, tokens, own, above, below, far,
    keep, keep_far, send, token_blocks, grads,
):
    gather_blocks(plane, dp_place, tokens, (own, above, below, far), token_blocks, grads)
    count = live_count[0, 0]
    core = lax.rem(dp_place[0, 0], 2)
    side = lax.div(dp_place[0, 0], 2)
    for n in range(index.shape[1]):
        from_core, from_side, spot = n // 16, n % 16 // 8, n % 8
        owner_core = core if from_core else 1 - core
        owner_side = side if from_side else 1 - side
        s = (owner_side * 2 + owner_core) * 8 + spot
        live = s < count
        product = lax.dot_general(
            grads[jnp.where(live, index[0, s], 0)],
            token_blocks[jnp.where(live, index[1, s], 0)],
            (((0,), (0,)), ((), ())),
            preferred_element_type=f32,
        )
        out = (keep if from_side else keep_far) if from_core else send.at[from_side]
        out[spot] = jnp.where(live, product * grad_scale, 0.0).astype(bf16)


def features_kernel(
    index, live_count, plane, dp_place, tokens, weights, own, above, below, far,
    kept, sent, token_blocks, grads, total,
):
    gather_blocks(plane, dp_place, tokens, (own, above, below, far), token_blocks, grads)
    cols = total.shape[0] - 1
    for m in range(cols):
        total[m] = jnp.zeros_like(total[m])
    for s in range(index.shape[1]):
        live = s < live_count[0, 0]
        total[jnp.where(live, index[1, s], cols)] += jnp.dot(
            grads[jnp.where(live, index[0, s], 0)], weights[s], preferred_element_type=f32
        )
    here = lax.rem(dp_place[0, 1], 2)
    for k in range(cols // 2):
        kept[k] = total[2 * k + here].astype(bf16)
        sent[k] = total[2 * k + 1 - here].astype(bf16)


def call(kernel, outs, scratch, flops, *operands):
    return pl.pallas_call(
        kernel,
        out_shape=[jax.ShapeDtypeStruct(s, bf16) for s in outs],
        in_specs=[pl.BlockSpec(memory_space=pltpu.SMEM)] * 4
        + [pl.BlockSpec(memory_space=pltpu.VMEM)] * (len(operands) - 4),
        out_specs=[pl.BlockSpec(memory_space=pltpu.VMEM)] * len(outs),
        scratch_shapes=[pltpu.VMEM(s, t) for s, t in scratch],
        compiler_params=pltpu.CompilerParams(vmem_limit_bytes=32 * 2**20),
        cost_estimate=pl.CostEstimate(flops=flops, bytes_accessed=flops // 256, transcendentals=0),
    )(*operands)


def sum_kernel(parts, out):
    total = parts[0].astype(f32)
    for n in range(1, parts.shape[0]):
        total += parts[n].astype(f32)
    out[...] = total.astype(bf16)


def call_sum(parts, flops):
    return pl.pallas_call(
        sum_kernel,
        out_shape=jax.ShapeDtypeStruct(parts.shape[1:], bf16),
        in_specs=[pl.BlockSpec(memory_space=pltpu.VMEM)],
        out_specs=pl.BlockSpec(memory_space=pltpu.VMEM),
        compiler_params=pltpu.CompilerParams(vmem_limit_bytes=8 * 2**20),
        cost_estimate=pl.CostEstimate(flops=flops, bytes_accessed=flops // 256, transcendentals=0),
    )(parts)


def shifted(x, axis, by):
    n = lax.axis_size(axis)
    return lax.ppermute(x, axis, [(i, (i + by) % n) for i in range(n)])


def both_ways(x, by):
    n, parts = lax.axis_size("col"), lax.axis_size("dp")
    pairs = []
    for i in range(n):
        for d in range(parts):
            to = (i + (by if d % 2 == 0 else -by)) % n
            pairs.append((i * parts + d, to * parts + d))
    return lax.ppermute(x, ("col", "dp"), pairs)


def swapped(x, axis, bit):
    return lax.ppermute(x, axis, [(i, i ^ bit) for i in range(lax.axis_size(axis))])


def summed(*parts):
    total = parts[0].astype(f32)
    for part in parts[1:]:
        total = total + part.astype(f32)
    return total.astype(bf16)


def local(tokens, block_values, block_index, block_count, grad_hidden):
    weights = block_values[0, 0]
    capacity = weights.shape[0]
    token_count = tokens.shape[0]
    col_blocks = tokens.shape[1] // block
    planes = lax.axis_size("col")
    rows = planes * (grad_hidden.shape[1] // block)
    place = lax.axis_index("col")
    dp = lax.axis_index("dp")
    quarter = (planes // 4, token_count, grad_hidden.shape[1])
    info = (block_index[0, 0], block_count, place.reshape(1, 1), jnp.stack([dp, lax.axis_index("row")])[None])
    blocks = (token_count, block)
    owned = (capacity // lax.axis_size("dp"), block, block)

    strided = [[i + 4 * j for j in range(planes // 4)] for i in range(4)]
    copies = jnp.broadcast_to(grad_hidden[None], quarter)
    grads_own = lax.all_to_all(copies, "col", 0, 0, tiled=True, axis_index_groups=strided)
    own, up, down, far = call(
        hidden_kernel,
        [quarter] * 4,
        [((col_blocks, *blocks), bf16), ((rows + 1, *blocks), f32)],
        2 * capacity * token_count * block * block,
        *info, tokens, weights,
    )
    from_far = both_ways(far, 2)
    from_below = shifted(up, "col", 1)
    from_above = shifted(down, "col", -1)
    grads_own, from_far, from_below, from_above = lax.optimization_barrier(
        (grads_own, from_far, from_below, from_above)
    )
    hidden_near = summed(own, from_far, from_below, from_above)
    hidden_parts = lax.all_to_all(hidden_near, "col", 0, 0, tiled=True, axis_index_groups=strided)
    above = shifted(grads_own, "col", -1)
    below = shifted(grads_own, "col", 1)
    across = both_ways(grads_own, 2)
    token_scratch = ((col_blocks, *blocks), bf16)
    grads_scratch = ((rows, *blocks), bf16)
    keep, keep_far, send = call(
        blocks_kernel,
        [owned, owned, (2, *owned)],
        [token_scratch, grads_scratch],
        low_cost,
        *info, tokens, grads_own, above, below, across,
    )
    received = swapped(send, "dp", 1)
    theirs = summed(keep_far, received[0])
    from_side = swapped(theirs, "dp", 2)
    kept, sent = call(
        features_kernel,
        [(col_blocks // 2, *blocks)] * 2,
        [token_scratch, grads_scratch, ((col_blocks + 1, *blocks), f32)],
        low_cost,
        *info, tokens, weights, grads_own, above, below, across,
    )
    features = summed(kept, swapped(sent, "row", 1))
    hidden = call_sum(hidden_parts, high_cost)
    features, hidden = lax.optimization_barrier((features, hidden))
    along_x = [list(range(i, col_blocks, 2)) for i in range(2)]
    feature_parts = lax.all_to_all(
        features, "row", 0, 0, tiled=True, axis_index_groups=along_x
    )
    grad_blocks = summed(keep, received[1], from_side)
    feature_parts, grad_blocks = lax.optimization_barrier((feature_parts, grad_blocks))
    grad_tokens = summed(*[feature_parts[i] for i in range(feature_parts.shape[0])])
    return hidden, grad_tokens, grad_blocks[None, None]


def solution(mesh):
    in_specs = (
        P("dp", "col"),
        P("row", "col", None, None, None),
        P("row", "col", None, None),
        P("row", "col"),
        P("dp", ("row", "col")),
    )
    out_specs = (
        P("dp", ("row", "col")),
        P("dp", ("col", "row")),
        P("row", "col", "dp", None, None),
    )
    return jax.shard_map(local, mesh=mesh, in_specs=in_specs, out_specs=out_specs, check_vma=False)
```

```python
import jax
import jax.numpy as jnp
from jax import lax
from jax.experimental import pallas as pl
from jax.experimental.pallas import tpu as pltpu
from jax.sharding import PartitionSpec as P

grad_scale = 0.0625
low_cost = 1000
high_cost = 8 * 10**9
block = 128
f32 = jnp.float32
bf16 = jnp.bfloat16


def hidden_kernel(
    index, live_count, plane, dp_place, tokens, weights, own, up, down, far, token_blocks, total
):
    capacity = weights.shape[0]
    rows = total.shape[0] - 1
    for m in range(token_blocks.shape[0]):
        token_blocks[m] = tokens[:, m * block : (m + 1) * block]
    for b in range(rows):
        total[b] = jnp.zeros_like(total[b])
    count = live_count[0, 0]
    place = plane[0, 0]
    for s in range(capacity):
        live = s < count
        row = jnp.where(live, index[0, s], rows)
        col = jnp.where(live, index[1, s], 0)
        total[row] += lax.dot_general(
            token_blocks[col], weights[s], (((1,), (1,)), ((), ())), preferred_element_type=f32
        )
    far_shift = 2 - 4 * lax.rem(dp_place[0, 0], 2)
    for shift, out in ((1, up), (-1, down), (far_shift, far), (0, own)):
        near = lax.rem(place + shift + 4, 4)
        for a in range(out.shape[0]):
            to = 4 * a + near
            for half in range(2):
                out[a, :, half * block : (half + 1) * block] = total[to * 2 + half].astype(bf16)


def gather_blocks(plane, dp_place, tokens, parts, token_blocks, grads):
    rows = grads.shape[0]
    for m in range(token_blocks.shape[0]):
        token_blocks[m] = tokens[:, m * block : (m + 1) * block]
    far_shift = 4 * lax.rem(dp_place[0, 0], 2) - 2
    for shift, part in zip((0, 1, -1, far_shift), parts):
        near = lax.rem(plane[0, 0] + shift + 4, 4)
        for a in range(part.shape[0]):
            at = 4 * a + near
            for half in range(2):
                grads[at * 2 + half] = part[a, :, half * block : (half + 1) * block]


def blocks_kernel(
    index, live_count, plane, dp_place, tokens, own, above, below, far,
    keep, keep_far, send, token_blocks, grads,
):
    gather_blocks(plane, dp_place, tokens, (own, above, below, far), token_blocks, grads)
    count = live_count[0, 0]
    core = lax.rem(dp_place[0, 0], 2)
    side = lax.div(dp_place[0, 0], 2)
    for n in range(index.shape[1]):
        from_core, from_side, spot = n // 16, n % 16 // 8, n % 8
        owner_core = core if from_core else 1 - core
        owner_side = side if from_side else 1 - side
        s = (owner_side * 2 + owner_core) * 8 + spot
        live = s < count
        product = lax.dot_general(
            grads[jnp.where(live, index[0, s], 0)],
            token_blocks[jnp.where(live, index[1, s], 0)],
            (((0,), (0,)), ((), ())),
            preferred_element_type=f32,
        )
        out = (keep if from_side else keep_far) if from_core else send.at[from_side]
        out[spot] = jnp.where(live, product * grad_scale, 0.0).astype(bf16)


def features_kernel(
    index, live_count, plane, dp_place, tokens, weights, own, above, below, far,
    kept, sent, token_blocks, grads, total,
):
    gather_blocks(plane, dp_place, tokens, (own, above, below, far), token_blocks, grads)
    cols = total.shape[0] - 1
    for m in range(cols):
        total[m] = jnp.zeros_like(total[m])
    for s in range(index.shape[1]):
        live = s < live_count[0, 0]
        total[jnp.where(live, index[1, s], cols)] += jnp.dot(
            grads[jnp.where(live, index[0, s], 0)], weights[s], preferred_element_type=f32
        )
    here = lax.rem(dp_place[0, 1], 2)
    for k in range(cols // 2):
        kept[k] = total[2 * k + here].astype(bf16)
        sent[k] = total[2 * k + 1 - here].astype(bf16)


def call(kernel, outs, scratch, flops, *operands):
    return pl.pallas_call(
        kernel,
        out_shape=[jax.ShapeDtypeStruct(s, bf16) for s in outs],
        in_specs=[pl.BlockSpec(memory_space=pltpu.SMEM)] * 4
        + [pl.BlockSpec(memory_space=pltpu.VMEM)] * (len(operands) - 4),
        out_specs=[pl.BlockSpec(memory_space=pltpu.VMEM)] * len(outs),
        scratch_shapes=[pltpu.VMEM(s, t) for s, t in scratch],
        compiler_params=pltpu.CompilerParams(vmem_limit_bytes=32 * 2**20),
        cost_estimate=pl.CostEstimate(flops=flops, bytes_accessed=flops // 256, transcendentals=0),
    )(*operands)


def sum_kernel(parts, out):
    total = parts[0].astype(f32)
    for n in range(1, parts.shape[0]):
        total += parts[n].astype(f32)
    out[...] = total.astype(bf16)


def call_sum(parts, flops):
    return pl.pallas_call(
        sum_kernel,
        out_shape=jax.ShapeDtypeStruct(parts.shape[1:], bf16),
        in_specs=[pl.BlockSpec(memory_space=pltpu.VMEM)],
        out_specs=pl.BlockSpec(memory_space=pltpu.VMEM),
        compiler_params=pltpu.CompilerParams(vmem_limit_bytes=8 * 2**20),
        cost_estimate=pl.CostEstimate(flops=flops, bytes_accessed=flops // 256, transcendentals=0),
    )(parts)


def shifted(x, axis, by):
    n = lax.axis_size(axis)
    return lax.ppermute(x, axis, [(i, (i + by) % n) for i in range(n)])


def both_ways(x, by):
    n, parts = lax.axis_size("col"), lax.axis_size("dp")
    pairs = []
    for i in range(n):
        for d in range(parts):
            to = (i + (by if d % 2 == 0 else -by)) % n
            pairs.append((i * parts + d, to * parts + d))
    return lax.ppermute(x, ("col", "dp"), pairs)


def swapped(x, axis, bit):
    return lax.ppermute(x, axis, [(i, i ^ bit) for i in range(lax.axis_size(axis))])


def summed(*parts):
    total = parts[0].astype(f32)
    for part in parts[1:]:
        total = total + part.astype(f32)
    return total.astype(bf16)


def local(tokens, block_values, block_index, block_count, grad_hidden):
    weights = block_values[0, 0]
    capacity = weights.shape[0]
    token_count = tokens.shape[0]
    col_blocks = tokens.shape[1] // block
    planes = lax.axis_size("col")
    rows = planes * (grad_hidden.shape[1] // block)
    place = lax.axis_index("col")
    dp = lax.axis_index("dp")
    quarter = (planes // 4, token_count, grad_hidden.shape[1])
    info = (block_index[0, 0], block_count, place.reshape(1, 1), jnp.stack([dp, lax.axis_index("row")])[None])
    blocks = (token_count, block)
    owned = (capacity // lax.axis_size("dp"), block, block)

    strided = [[i + 4 * j for j in range(planes // 4)] for i in range(4)]
    copies = jnp.broadcast_to(grad_hidden[None], quarter)
    grads_own = lax.all_to_all(copies, "col", 0, 0, tiled=True, axis_index_groups=strided)
    own, up, down, far = call(
        hidden_kernel,
        [quarter] * 4,
        [((col_blocks, *blocks), bf16), ((rows + 1, *blocks), f32)],
        2 * capacity * token_count * block * block,
        *info, tokens, weights,
    )
    from_far = both_ways(far, 2)
    from_below = shifted(up, "col", 1)
    from_above = shifted(down, "col", -1)
    grads_own, from_far, from_below, from_above = lax.optimization_barrier(
        (grads_own, from_far, from_below, from_above)
    )
    hidden_near = summed(own, from_far, from_below, from_above)
    hidden_parts = lax.all_to_all(hidden_near, "col", 0, 0, tiled=True, axis_index_groups=strided)
    above = shifted(grads_own, "col", -1)
    below = shifted(grads_own, "col", 1)
    across = both_ways(grads_own, 2)
    token_scratch = ((col_blocks, *blocks), bf16)
    grads_scratch = ((rows, *blocks), bf16)
    keep, keep_far, send = call(
        blocks_kernel,
        [owned, owned, (2, *owned)],
        [token_scratch, grads_scratch],
        low_cost,
        *info, tokens, grads_own, above, below, across,
    )
    received = swapped(send, "dp", 1)
    theirs = summed(keep_far, received[0])
    kept, sent = call(
        features_kernel,
        [(col_blocks // 2, *blocks)] * 2,
        [token_scratch, grads_scratch, ((col_blocks + 1, *blocks), f32)],
        low_cost,
        *info, tokens, weights, grads_own, above, below, across,
    )
    sent, theirs = lax.optimization_barrier((sent, theirs))
    from_side = swapped(theirs, "dp", 2)
    features = summed(kept, swapped(sent, "row", 1))
    hidden = call_sum(hidden_parts, high_cost)
    features, hidden = lax.optimization_barrier((features, hidden))
    along_x = [list(range(i, col_blocks, 2)) for i in range(2)]
    feature_parts = lax.all_to_all(
        features, "row", 0, 0, tiled=True, axis_index_groups=along_x
    )
    grad_blocks = summed(keep, received[1], from_side)
    feature_parts, grad_blocks = lax.optimization_barrier((feature_parts, grad_blocks))
    grad_tokens = summed(*[feature_parts[i] for i in range(feature_parts.shape[0])])
    return hidden, grad_tokens, grad_blocks[None, None]


def solution(mesh):
    in_specs = (
        P("dp", "col"),
        P("row", "col", None, None, None),
        P("row", "col", None, None),
        P("row", "col"),
        P("dp", ("row", "col")),
    )
    out_specs = (
        P("dp", ("row", "col")),
        P("dp", ("col", "row")),
        P("row", "col", "dp", None, None),
    )
    return jax.shard_map(local, mesh=mesh, in_specs=in_specs, out_specs=out_specs, check_vma=False)
```
